256 devices in a mesh: rep: 8 (over x_lo, y), tp: 32 (over x_hi, z, core).
Axes of the slice: x: 4 (x_hi: 2, x_lo: 2; x = x_hi * 2 + x_lo), y: 4, z: 8, core: 2. Of those that a mesh axis runs over, the one named last changes fastest.
Arguments:
- inputs: bfloat16 [4096, 8192], P(('rep', 'tp')), may hold values from -20 to 20
- heads_out: bfloat16 [4096, 4096], P('rep', 'tp'), may hold values from -6 to 6
- out_weight: bfloat16 [4096, 8192], P('tp'), may hold values from -0.09375 to 0.09375
- norm_gain: float32 [8192], replicated, may hold values from 0.25 to 1.75
- cotangent: bfloat16 [4096, 8192], P(('rep', 'tp')), may hold values from -6 to 6
- inner_params: float32 [8, 8388608], P('rep', 'tp'), may hold values from -6 to 6
- outer_base: float32 [8388608], P('tp'), may hold values from -6 to 6
- momentum: float32 [32, 8, 32768], P('tp', 'rep'), may hold values from -3 to 3
Outputs:
- d_resid: bfloat16 [4096, 8192], P(('rep', 'tp'))
- d_heads: bfloat16 [4096, 4096], P('rep', 'tp')
- d_out_weight: bfloat16 [8, 4096, 8192], P('rep', 'tp')
- new_base: float32 [8388608], P('tp')
- new_momentum: float32 [32, 8, 32768], P('tp', 'rep')
The draws below stay inside these ranges and needn't reach their ends.
All inputs are finite; a program needn't handle non-finite values.
Results may differ from the reference program's by a relative error of at most 0.035.
Values may be sent and summed in bfloat16 or wider, within the bound.
No kernel may reach another device: no remote copies, remote signals or barrier semaphores. Data moves between devices by JAX's collectives and lax.ppermute only.
A program may use at most 128 MiB of HBM per device.

```python
import jax
import jax.numpy as jnp
from jax import lax

D = 8192
HEADS = 32
HD = 128
GROUP_TOKENS = 512
TOKENS = 4096
FRAG = 8388608
SHARE = 32768
N_REP = 8
N_TP = 32


def shared_base(key):
    key = jax.random.fold_in(key, 41)
    normal_key = jax.random.fold_in(key, 0)
    normal_values = jax.random.truncated_normal(normal_key, -4.0, 4.0, (TOKENS, D), jnp.float32)
    return normal_values


def draw_inputs(key, part):
    normal_values = shared_base(key)
    key = jax.random.fold_in(key, 11)
    col_key, row_key = jax.random.split(key)
    col_scale = 0.15 * 10.0 ** jax.random.uniform(col_key, (D,), jnp.float32, 0.0, 1.0)
    values = normal_values
    row_scale = 10.0 ** jax.random.uniform(row_key, (TOKENS, 1), jnp.float32, -0.5, 0.5)
    return (values * row_scale * col_scale[None, :]).astype(jnp.bfloat16)


def draw_cotangent(key, part):
    normal_values = shared_base(key)
    key = jax.random.fold_in(key, 23)
    values = normal_values
    noise = jax.random.truncated_normal(key, -4.0, 4.0, (TOKENS, D), jnp.float32)
    return (0.8 * values + 0.6 * noise).astype(jnp.bfloat16)


def with_spikes(drawn, own_key, source, target, parts, factor):
    def block_of(axis_at):
        return (jnp.arange(drawn.shape[axis_at]) // (drawn.shape[axis_at] // parts)).reshape((-1,) + (1,) * (drawn.ndim - 1 - axis_at))

    near = jax.random.permutation(own_key, parts)[block_of(target)]
    other_side = (block_of(target) + parts // 2) % parts
    return jnp.where((block_of(source) == near) | (block_of(source) == other_side), factor * drawn, drawn)


def level_of(stream_key, shape, pieces, low, largest):
    def one(position, blocks):
        draws = jax.random.uniform(jax.random.fold_in(jax.random.fold_in(stream_key, 6), position), (blocks,), jnp.float32, low / len(pieces), largest / len(pieces))
        return jnp.repeat(jnp.exp(draws), shape[position] // blocks).reshape((-1,) + (1,) * (len(shape) - position - 1))

    factor_of = one(*pieces[0])
    for cut in pieces[1:]:
        factor_of = factor_of * one(*cut)
    return factor_of


def centred(key, shape, scale, limit, cuts=(), kind=jnp.bfloat16):
    factor_of = level_of(key, shape, cuts, -0.22, 0.18) if cuts else 1.0
    drawn = jax.random.normal(key, shape, jnp.float32) * scale * factor_of
    return jnp.minimum(jnp.maximum(drawn, -limit), limit).astype(kind)


def bell_draw_with(stream_key, shape, width, bound, pieces, heavy, dtype=jnp.bfloat16):
    result = width * jax.random.normal(stream_key, shape, jnp.float32)
    if pieces:
        result = result * level_of(stream_key, shape, pieces, -0.22, 0.18)
    return jnp.clip(with_spikes(result, jax.random.fold_in(stream_key, 3), *heavy), -bound, bound).astype(dtype)


def setup_inputs(seed: int = 0) -> dict:
    seeds = jax.random.split(jax.random.key(seed), 9)
    return {
        "inputs": draw_inputs(jax.random.fold_in(seeds[8], 71), 0),
        "heads_out": centred(seeds[1], (TOKENS, HEADS * HD), 1.0, 6.0, ((0, 8), (1, 32))),
        "out_weight": centred(seeds[2], (HEADS * HD, D), (HEADS * HD) ** -0.5, 0.09375, ((0, 32),)),
        "norm_gain": jnp.clip(1.0 + 0.15 * jax.random.normal(seeds[3], (D,), jnp.float32), 0.25, 1.75),
        "cotangent": draw_cotangent(jax.random.fold_in(seeds[8], 71), 0),
        "inner_params": bell_draw_with(seeds[5], (N_REP, FRAG), 1.0, 6.0, ((0, 8), (1, 32)), (0, 1, 8, 2.0), jnp.float32),
        "outer_base": centred(seeds[6], (FRAG,), 1.0, 6.0, ((0, 32),), jnp.float32),
        "momentum": centred(seeds[7], (N_TP, N_REP, SHARE), 0.5, 3.0, ((0, 32), (1, 8)), jnp.float32),
    }


norm_eps = 1e-05
outer_rate = 0.7
momentum_coef = 0.9

def group_pass(operands, out_weight, norm_gain):
    heads_rows, input_rows, cot_rows = operands
    residual_sum = input_rows.astype(jnp.float32) + jnp.dot(heads_rows, out_weight, preferred_element_type=jnp.float32)
    inv_rms = lax.rsqrt(lax.optimization_barrier(jnp.mean(residual_sum * residual_sum, axis=-1, keepdims=True)) + norm_eps)
    scaled = norm_gain[None, :] * cot_rows.astype(jnp.float32)
    inner_mean = lax.optimization_barrier(jnp.mean(scaled * residual_sum, axis=-1, keepdims=True))
    d_resid = (inv_rms * scaled - residual_sum * inv_rms ** 3 * inner_mean).astype(jnp.bfloat16)
    d_heads = lax.dot_general(d_resid, out_weight, (((1,), (1,)), ((), ())), preferred_element_type=jnp.float32).astype(jnp.bfloat16)
    d_weight = lax.dot_general(heads_rows, d_resid, (((0,), (0,)), ((), ())), preferred_element_type=jnp.float32).astype(jnp.bfloat16)
    return (d_resid, d_heads, d_weight)

def reference(inputs, heads_out, out_weight, norm_gain, cotangent, inner_params, outer_base, momentum):
    group_heads = heads_out.reshape(N_REP, GROUP_TOKENS, HEADS * HD)
    group_inputs = inputs.reshape(N_REP, GROUP_TOKENS, D)
    group_cot = cotangent.reshape(N_REP, GROUP_TOKENS, D)
    d_resid, d_heads, d_out_weight = lax.map(lambda ops: group_pass(ops, out_weight, norm_gain), (group_heads, group_inputs, group_cot))
    difference = (outer_base[None, :] - inner_params).astype(jnp.bfloat16)
    mean_delta = lax.optimization_barrier(jnp.sum(difference.astype(jnp.float32), axis=0)) / N_REP
    mean_delta = mean_delta.reshape(N_TP, N_REP, SHARE)
    new_momentum = momentum_coef * momentum + mean_delta
    outer_step = (outer_rate * (mean_delta + momentum_coef * new_momentum)).astype(jnp.bfloat16)
    new_base = outer_base - outer_step.astype(jnp.float32).reshape(FRAG)
    return (d_resid.reshape(TOKENS, D), d_heads.reshape(TOKENS, HEADS * HD), d_out_weight, new_base, new_momentum)
```

```python
import jax
import jax.numpy as jnp
from jax import lax
from jax.sharding import Mesh
from jax.sharding import PartitionSpec as P

norm_eps = 1e-05
outer_rate = 0.7
momentum_coef = 0.9

AXES = ("xl", "y", "xh", "z", "c")
REP = ("xl", "y")
F32 = jnp.float32
BF16 = jnp.bfloat16
STREAMS = 2
NZ = 8


def shift(x, axis, step):
    n = lax.axis_size(axis)
    return lax.ppermute(x, axis, [(i, (i + step) % n) for i in range(n)])


def swap(x, axis):
    return shift(x, axis, 1)


def dot(a, b):
    return jnp.dot(a, b, preferred_element_type=F32)


def halves(x, c):
    n = x.shape[1] // 2
    mine = lax.dynamic_slice_in_dim(x, c * n, n, 1)
    other = lax.dynamic_slice_in_dim(x, (1 - c) * n, n, 1)
    return mine, other


def joined(mine, other, c):
    first = jnp.where(c == 0, mine, other)
    second = jnp.where(c == 0, other, mine)
    return jnp.concatenate([first, second], axis=1)


def ring_reduce(rows, weight):
    half = weight.shape[1] // 2

    def part(j, w):
        return dot(rows[j], w)

    up = part(4, weight[:, :half]).astype(BF16)
    down = part(4, weight[:, half:]).astype(BF16)
    up = shift(up, "z", 1)
    down = shift(down, "z", -1)
    for j in (3, 2, 1):
        at_up, at_down = part(j, weight), part(8 - j, weight)
        if j == 3:
            at_up = jnp.concatenate([at_up[:, :half] + up.astype(F32), at_up[:, half:]], axis=1)
            at_down = jnp.concatenate([at_down[:, :half], at_down[:, half:] + down.astype(F32)], axis=1)
        else:
            at_up = at_up + up.astype(F32)
            at_down = at_down + down.astype(F32)
        up = shift(at_up.astype(BF16), "z", 1)
        down = shift(at_down.astype(BF16), "z", -1)
    return part(0, weight) + up.astype(F32) + down.astype(F32)


def ring_gather(own):
    half = own.shape[1] // 2
    got = [own] + [None] * 7
    up = down = own
    for j in (1, 2, 3):
        up = shift(up, "z", 1)
        down = shift(down, "z", -1)
        got[8 - j], got[j] = up, down
    left = shift(up[:, :half], "z", 1)
    right = shift(down[:, half:], "z", -1)
    got[4] = jnp.concatenate([left, right], axis=1)
    return got


def inner_work(inputs, heads_out, out_weight, norm_gain, cotangent):
    c, z, xh = lax.axis_index("c"), lax.axis_index("z"), lax.axis_index("xh")
    tokens, width = heads_out.shape
    d = out_weight.shape[1]
    share = tokens // (2 * NZ)
    weight_mine, weight_other = halves(out_weight, c)
    weight = jnp.concatenate([weight_mine, swap(weight_other, "c")], axis=0)
    heads = jnp.concatenate([heads_out, swap(heads_out, "c")], axis=1)
    by_z = heads.reshape(2, NZ, share, 2 * width)
    rolled = lax.dynamic_slice_in_dim(jnp.concatenate([by_z, by_z], axis=1), z, NZ, 1)
    rolled = rolled.transpose(1, 0, 2, 3).reshape(NZ, 2 * share, 2 * width)

    cols = weight.shape[1] // STREAMS
    pieces = [
        ring_reduce([rolled[j] for j in range(NZ)], weight[:, s * cols : (s + 1) * cols])
        for s in range(STREAMS)
    ]
    summed = []
    for piece in pieces:
        mine = lax.dynamic_slice_in_dim(piece, xh * share, share, 0)
        other = lax.dynamic_slice_in_dim(piece, (1 - xh) * share, share, 0)
        summed.append(mine + swap(other.astype(BF16), "xh").astype(F32))
    summed = jnp.concatenate(summed, axis=1)
    rows = share // 2
    mine = lax.dynamic_slice_in_dim(summed, c * rows, rows, 0)
    other = lax.dynamic_slice_in_dim(summed, (1 - c) * rows, rows, 0)
    summed = joined(mine, swap(other.astype(BF16), "c").astype(F32), c)

    residual_sum = inputs.astype(F32) + summed
    inv_rms = lax.rsqrt(jnp.mean(residual_sum * residual_sum, axis=-1, keepdims=True) + norm_eps)
    scaled = norm_gain[None, :] * cotangent.astype(F32)
    inner_mean = jnp.mean(scaled * residual_sum, axis=-1, keepdims=True)
    d_resid = (inv_rms * scaled - residual_sum * inv_rms**3 * inner_mean).astype(BF16)

    def ordered(mine, other, at):
        return jnp.concatenate([jnp.where(at == 0, mine, other), jnp.where(at == 0, other, mine)], axis=0)

    mine, other = halves(d_resid, c)
    chip_rows = ordered(mine, swap(other, "c"), c)
    pair_rows = ordered(chip_rows, swap(chip_rows, "xh"), xh)
    gathered = [ring_gather(pair_rows[:, s * cols : (s + 1) * cols]) for s in range(STREAMS)]
    shard = jnp.concatenate([jnp.concatenate(g, axis=0) for g in gathered], axis=1)

    flat = rolled.reshape(tokens, 2 * width)
    weight_grad = lax.dot_general(flat, shard, (((0,), (0,)), ((), ())), preferred_element_type=F32).astype(BF16)
    weight_grad = joined(weight_grad[:width], swap(weight_grad[width:], "c"), c)
    head_rows = lax.dot_general(shard, weight, (((1,), (1,)), ((), ())), preferred_element_type=F32)
    head_rows = head_rows[:, :width] + swap(head_rows[:, width:].astype(BF16), "c").astype(F32)
    head_rows = head_rows.astype(BF16).reshape(NZ, 2, share, width).transpose(1, 0, 2, 3)
    head_rows = lax.dynamic_slice_in_dim(jnp.concatenate([head_rows, head_rows], axis=1), (NZ - z) % NZ, NZ, 1)
    return d_resid, head_rows.reshape(tokens, width), weight_grad[None]


def outer_work(inner_params, outer_base, momentum):
    replicas = lax.axis_size("xl") * lax.axis_size("y")
    shape = (replicas, outer_base.shape[0] // (replicas * 128), 128)
    base = outer_base.reshape(shape)
    difference = (base - inner_params.reshape(shape)).astype(BF16)
    parts = lax.all_to_all(difference, REP, 0, 0, tiled=True)
    mean_delta = jnp.sum(parts.astype(F32), axis=0) / replicas
    new_momentum = momentum_coef * momentum.reshape(shape[1:]) + mean_delta
    outer_step = (outer_rate * (mean_delta + momentum_coef * new_momentum)).astype(BF16)
    steps = lax.all_gather(outer_step, REP, axis=0, tiled=False)
    new_base = (base - steps.astype(F32)).reshape(outer_base.shape)
    return new_base, new_momentum.reshape(momentum.shape)


def per_device(inputs, heads_out, out_weight, norm_gain, cotangent, inner_params, outer_base, momentum):
    new_base, new_momentum = outer_work(inner_params, outer_base, momentum)
    d_resid, d_heads, d_out_weight = inner_work(inputs, heads_out, out_weight, norm_gain, cotangent)
    return d_resid, d_heads, d_out_weight, new_base, new_momentum


def solution(mesh):
    fine = Mesh(mesh.devices.reshape(2, 4, 2, NZ, 2), AXES)
    rep, tp = REP, ("xh", "z", "c")
    return jax.shard_map(
        per_device,
        mesh=fine,
        in_specs=(
            P(AXES, None),
            P(rep, tp),
            P(tp, None),
            P(),
            P(AXES, None),
            P(rep, tp),
            P(tp),
            P(tp, rep, None),
        ),
        out_specs=(P(AXES, None), P(rep, tp), P(rep, tp, None), P(tp), P(tp, rep, None)),
        check_vma=False,
    )
```

```python
import jax
import jax.numpy as jnp
from jax import lax
from jax.sharding import Mesh
from jax.sharding import PartitionSpec as P

norm_eps = 1e-05
outer_rate = 0.7
momentum_coef = 0.9

AXES = ("xl", "y", "xh", "z", "c")
REP = ("xl", "y")
F32 = jnp.float32
BF16 = jnp.bfloat16
NZ = 8
STREAMS = 2


def shift(x, axis, step):
    n = lax.axis_size(axis)
    return lax.ppermute(x, axis, [(i, (i + step) % n) for i in range(n)])


def swap(x, axis):
    return shift(x, axis, 1)


def dot(a, b):
    return jnp.dot(a, b, preferred_element_type=F32)


def together(*xs):
    return lax.optimization_barrier(xs)


def relative(x, axis, at):
    return lax.dynamic_slice_in_dim(jnp.concatenate([x, x], axis=axis), at, x.shape[axis], axis)


def absolute(x, axis, at):
    n = x.shape[axis]
    return lax.dynamic_slice_in_dim(jnp.concatenate([x, x], axis=axis), (n - at) % n, n, axis)


def halves(x, c):
    n = x.shape[-1] // 2
    mine = lax.dynamic_slice_in_dim(x, c * n, n, x.ndim - 1)
    other = lax.dynamic_slice_in_dim(x, (1 - c) * n, n, x.ndim - 1)
    return mine, other


def joined(mine, other, c):
    first = jnp.where(c == 0, mine, other)
    second = jnp.where(c == 0, other, mine)
    return jnp.concatenate([first, second], axis=1)


def reduce_step(up, down, at_up, at_down, step):
    half = at_up.shape[1] // 2
    if step == 4:
        at_up, at_down = at_up[:, :half], at_down[:, half:]
    elif step == 3:
        at_up = jnp.concatenate([at_up[:, :half] + up.astype(F32), at_up[:, half:]], axis=1)
        at_down = jnp.concatenate([at_down[:, :half], at_down[:, half:] + down.astype(F32)], axis=1)
    else:
        at_up = at_up + up.astype(F32)
        at_down = at_down + down.astype(F32)
    return shift(at_up.astype(BF16), "z", 1), shift(at_down.astype(BF16), "z", -1)


def ring_reduce(rows, weight, beside=lambda j, sent: sent):
    up = down = None
    for j in (4, 3, 2, 1):
        up, down = reduce_step(up, down, dot(rows[j], weight), dot(rows[8 - j], weight), j)
        up = beside(j, up)
    total = dot(rows[0], weight) + up.astype(F32) + down.astype(F32)
    share = total.shape[0] // 2
    return total[:share] + swap(total[share:].astype(BF16), "xh").astype(F32)


def ring_gather(own, beside=lambda j, sent: sent):
    own = jnp.concatenate([own, swap(own, "xh")], axis=0)
    half = own.shape[1] // 2
    got = [own] + [None] * 7
    up = down = own
    for j in (1, 2, 3):
        up = shift(up, "z", 1)
        down = shift(down, "z", -1)
        up = beside(j, up)
        got[8 - j], got[j] = up, down
    left = shift(up[:, :half], "z", 1)
    right = shift(down[:, half:], "z", -1)
    got[4] = jnp.concatenate([left, right], axis=1)
    return jnp.concatenate(got, axis=0)


def own_first(x, bits):
    for axis, bit in enumerate(bits):
        x = jnp.where(bit == 0, x, jnp.flip(x, axis))
    return x


def swap_y(x, bit):
    return lax.ppermute(x, "y", [(i, i ^ bit) for i in range(4)])


def per_device(inputs, heads_out, out_weight, norm_gain, cotangent, inner_params, outer_base, momentum):
    c, z, xh = lax.axis_index("c"), lax.axis_index("z"), lax.axis_index("xh")
    tokens, width = heads_out.shape
    d = out_weight.shape[1]
    share = tokens // (2 * NZ)
    p = d // 2 // STREAMS
    cuts = [slice(s * p, (s + 1) * p) for s in range(STREAMS)]

    replicas = lax.axis_size("xl") * lax.axis_size("y")
    block = (2, 2, 2, outer_base.shape[0] // (replicas * 128), 128)
    xl, y = lax.axis_index("xl"), lax.axis_index("y")
    bits = (xl, y // 2, y % 2)
    base = outer_base.reshape(block)
    momentum_rows = momentum.reshape(block[3:])
    difference = own_first((base - inner_params.reshape(block)).astype(BF16), bits)
    work = {"x": swap(difference[1], "xl")}

    def beside_reduce(j, up):
        if j == 3:
            up, work["x"] = together(up, work["x"])
            work["pair"] = difference[0].astype(F32) + work["x"].astype(F32)
            work["y"] = swap_y(work["pair"][:, 1].astype(BF16), 1)
        elif j == 1:
            up, work["y"] = together(up, work["y"])
            quad = work["pair"][:, 0] + work["y"].astype(F32)
            total = quad[0] + swap_y(quad[1].astype(BF16), 2).astype(F32)
            mean_delta = total / replicas
            new_momentum = momentum_coef * momentum_rows + mean_delta
            work["momentum"] = new_momentum
            work["step"] = (outer_rate * (mean_delta + momentum_coef * new_momentum)).astype(BF16)
        return up

    def beside_gather(j, up):
        if j == 1:
            up, work["two"] = together(up, work["two"])
            work["four"] = jnp.stack([work["two"], swap_y(work["two"], 1)], axis=1)
        elif j == 3:
            up, work["four"] = together(up, work["four"])
            work["eight"] = jnp.stack([work["four"], swap(work["four"], "xl")])
        return up

    def both_rows(x):
        mine, other = halves(x, c)
        return jnp.concatenate([mine, swap(other, "c")], axis=0)

    weight_mine, weight_other = halves(out_weight, c)
    weight = jnp.concatenate([weight_mine, swap(weight_other, "c")], axis=0)
    heads = jnp.concatenate([heads_out, swap(heads_out, "c")], axis=1)
    by_x = heads.reshape(2, NZ, 2, share // 2, 2 * width)
    by_x = relative(relative(by_x, 0, xh), 2, c).reshape(2, NZ, share, 2 * width)
    by_z = relative(by_x, 1, z).transpose(1, 0, 2, 3).reshape(NZ, 2 * share, 2 * width)
    inputs, cotangent = both_rows(inputs), both_rows(cotangent)
    gain = halves(norm_gain, c)[0]

    rows = [by_z[j] for j in range(NZ)]
    rows[3], inputs, cotangent = together(rows[3], inputs, cotangent)
    pieces = [ring_reduce(rows, weight[:, cut], *([] if s else [beside_reduce])) for s, cut in enumerate(cuts)]

    residuals = [inputs[:, s].astype(F32) + piece for s, piece in zip(cuts, pieces)]
    scaled = [gain[None, s] * cotangent[:, s].astype(F32) for s in cuts]
    squares = sum(jnp.sum(r * r, axis=1) for r in residuals)
    products = sum(jnp.sum(r * s, axis=1) for r, s in zip(residuals, scaled))
    stats, work["step"] = together(jnp.stack([squares, products]), work["step"])
    work["two"] = jnp.stack([work["step"], swap_y(work["step"], 2)])
    other_stats = swap(stats, "c")
    other_stats = jnp.concatenate([other_stats[:, share // 2 :], other_stats[:, : share // 2]], axis=1)
    means = (stats + other_stats) / d
    inv_rms = lax.rsqrt(means[0] + norm_eps)[:, None]
    pull = inv_rms**3 * means[1][:, None]
    grads = [(inv_rms * s - r * pull).astype(BF16) for r, s in zip(residuals, scaled)]

    full = [ring_gather(g, *([] if s else [beside_gather])) for s, g in enumerate(grads)]
    outer_step = own_first(work["eight"], bits)
    new_base = (base - outer_step.astype(F32)).reshape(outer_base.shape)

    grad_rows = jnp.concatenate(grads, axis=1)
    d_resid = joined(grad_rows[: share // 2], swap(grad_rows[share // 2 :], "c"), c)

    flat = by_z.reshape(tokens, 2 * width)

    def weight_part(rows, grad):
        return lax.dot_general(rows, grad, (((0,), (0,)), ((), ())), preferred_element_type=F32).astype(BF16)

    def heads_part(grad, span):
        return lax.dot_general(grad, weight[:, span], (((1,), (1,)), ((), ())), preferred_element_type=F32)

    grads_w = [weight_part(flat, g) for g in full]
    others = [swap(g[width:], "c") for g in grads_w]
    weight_grad = joined(
        jnp.concatenate([g[:width] for g in grads_w], axis=1), jnp.concatenate(others, axis=1), c
    )
    head_rows = sum(heads_part(g, s) for g, s in zip(full, cuts))
    head_rows = absolute(head_rows.reshape(NZ, 2, share, 2 * width).transpose(1, 0, 2, 3), 1, z)
    head_rows = absolute(absolute(head_rows.reshape(2, NZ, 2, share // 2, 2 * width), 0, xh), 2, c)
    head_rows = head_rows.reshape(tokens, 2 * width)
    d_heads = (head_rows[:, :width] + swap(head_rows[:, width:].astype(BF16), "c").astype(F32)).astype(BF16)
    return d_resid, d_heads, weight_grad[None], new_base, work["momentum"].reshape(momentum.shape)


def solution(mesh):
    fine = Mesh(mesh.devices.reshape(2, 4, 2, NZ, 2), AXES)
    rep, tp = REP, ("xh", "z", "c")
    return jax.shard_map(
        per_device,
        mesh=fine,
        in_specs=(
            P(AXES, None),
            P(rep, tp),
            P(tp, None),
            P(),
            P(AXES, None),
            P(rep, tp),
            P(tp),
            P(tp, rep, None),
        ),
        out_specs=(P(AXES, None), P(rep, tp), P(rep, tp, None), P(tp), P(tp, rep, None)),
        check_vma=False,
    )
```

```python
import jax
import jax.numpy as jnp
from jax import lax
from jax.sharding import Mesh
from jax.sharding import PartitionSpec as P

norm_eps = 1e-05
outer_rate = 0.7
momentum_coef = 0.9

AXES = ("xl", "y", "xh", "z", "c")
REP = ("xl", "y")
F32 = jnp.float32
BF16 = jnp.bfloat16
NZ = 8
STREAMS = 2


def shift(x, axis, step):
    n = lax.axis_size(axis)
    return lax.ppermute(x, axis, [(i, (i + step) % n) for i in range(n)])


def swap(x, axis):
    return shift(x, axis, 1)


def dot(a, b):
    return jnp.dot(a, b, preferred_element_type=F32)


def together(*xs):
    return lax.optimization_barrier(xs)


def relative(x, axis, at):
    return lax.dynamic_slice_in_dim(jnp.concatenate([x, x], axis=axis), at, x.shape[axis], axis)


def absolute(x, axis, at):
    n = x.shape[axis]
    return lax.dynamic_slice_in_dim(jnp.concatenate([x, x], axis=axis), (n - at) % n, n, axis)


def my_half(x, c):
    n = x.shape[-1] // 2
    return lax.dynamic_slice_in_dim(x, c * n, n, x.ndim - 1)


def joined(mine, other, c):
    first = jnp.where(c == 0, mine, other)
    second = jnp.where(c == 0, other, mine)
    return jnp.concatenate([first, second], axis=1)


def reduce_step(up, down, at_up, at_down, step):
    half = at_up.shape[1] // 2
    if step == 4:
        at_up, at_down = at_up[:, :half], at_down[:, half:]
    elif step == 3:
        at_up = jnp.concatenate([at_up[:, :half] + up.astype(F32), at_up[:, half:]], axis=1)
        at_down = jnp.concatenate([at_down[:, :half], at_down[:, half:] + down.astype(F32)], axis=1)
    else:
        at_up = at_up + up.astype(F32)
        at_down = at_down + down.astype(F32)
    return shift(at_up.astype(BF16), "z", 1), shift(at_down.astype(BF16), "z", -1)


def ring_reduce(rows, weight, beside=lambda j, sent: sent):
    up = down = None
    for j in (4, 3, 2, 1):
        up, down = reduce_step(up, down, dot(rows[j], weight), dot(rows[8 - j], weight), j)
        up = beside(j, up)
    total = dot(rows[0], weight) + up.astype(F32) + down.astype(F32)
    share = total.shape[0] // 2
    return total[:share] + swap(total[share:].astype(BF16), "xh").astype(F32)


def ring_gather(own, beside=lambda j, sent: sent):
    own = jnp.concatenate([own, swap(own, "xh")], axis=0)
    half = own.shape[1] // 2
    got = [own] + [None] * 7
    up = down = own
    for j in (1, 2, 3):
        up = shift(up, "z", 1)
        down = shift(down, "z", -1)
        up = beside(j, up)
        got[8 - j], got[j] = up, down
    left = shift(up[:, :half], "z", 1)
    right = shift(down[:, half:], "z", -1)
    got[4] = jnp.concatenate([left, right], axis=1)
    return jnp.concatenate(got, axis=0)


def own_first(x, bits):
    for axis, bit in enumerate(bits):
        x = jnp.where(bit == 0, x, jnp.flip(x, axis))
    return x


def swap_y(x, bit):
    return lax.ppermute(x, "y", [(i, i ^ bit) for i in range(4)])


def per_device(inputs, heads_out, out_weight, norm_gain, cotangent, inner_params, outer_base, momentum):
    c, z, xh = lax.axis_index("c"), lax.axis_index("z"), lax.axis_index("xh")
    tokens, width = heads_out.shape
    d = out_weight.shape[1]
    share = tokens // (2 * NZ)
    p = d // 2 // STREAMS
    cuts = [slice(s * p, (s + 1) * p) for s in range(STREAMS)]

    replicas = lax.axis_size("xl") * lax.axis_size("y")
    block = (2, 2, 2, outer_base.shape[0] // (replicas * 128), 128)
    xl, y = lax.axis_index("xl"), lax.axis_index("y")
    bits = (xl, y // 2, y % 2)
    base = outer_base.reshape(block)
    momentum_rows = momentum.reshape(block[3:])
    difference = own_first((base - inner_params.reshape(block)).astype(BF16), bits)
    work = {"x": swap(difference[1], "xl")}

    def beside_reduce(j, up):
        if j == 3:
            up, work["x"] = together(up, work["x"])
            work["pair"] = difference[0].astype(F32) + work["x"].astype(F32)
            work["y"] = swap_y(work["pair"][:, 1].astype(BF16), 1)
        elif j == 1:
            up, work["y"] = together(up, work["y"])
            quad = work["pair"][:, 0] + work["y"].astype(F32)
            total = quad[0] + swap_y(quad[1].astype(BF16), 2).astype(F32)
            mean_delta = total / replicas
            new_momentum = momentum_coef * momentum_rows + mean_delta
            work["momentum"] = new_momentum
            work["step"] = (outer_rate * (mean_delta + momentum_coef * new_momentum)).astype(BF16)
        return up

    def beside_gather(j, up):
        if j == 1:
            up, work["two"] = together(up, work["two"])
            work["four"] = jnp.stack([work["two"], swap_y(work["two"], 1)], axis=1)
        elif j == 3:
            up, work["four"] = together(up, work["four"])
            work["eight"] = jnp.stack([work["four"], swap(work["four"], "xl")])
        return up

    def both_rows(mine, other):
        return jnp.concatenate([my_half(mine, c), my_half(other, c)], axis=0)

    weight = both_rows(out_weight, swap(out_weight, "c"))
    heads = jnp.concatenate([heads_out, swap(heads_out, "c")], axis=1)
    by_x = heads.reshape(2, NZ, 2, share // 2, 2 * width)
    by_x = relative(relative(by_x, 0, xh), 2, c).reshape(2, NZ, share, 2 * width)
    by_z = relative(by_x, 1, z).transpose(1, 0, 2, 3).reshape(NZ, 2 * share, 2 * width)
    other_inputs, other_cotangent = swap(inputs, "c"), swap(cotangent, "c")
    gain = my_half(norm_gain, c)

    rows = [by_z[j] for j in range(NZ)]
    rows[3], other_inputs, other_cotangent = together(rows[3], other_inputs, other_cotangent)
    pieces = [ring_reduce(rows, weight[:, cut], *([] if s else [beside_reduce])) for s, cut in enumerate(cuts)]

    inputs, cotangent = both_rows(inputs, other_inputs), both_rows(cotangent, other_cotangent)
    residuals = [inputs[:, s].astype(F32) + piece for s, piece in zip(cuts, pieces)]
    scaled = [gain[None, s] * cotangent[:, s].astype(F32) for s in cuts]
    squares = sum(jnp.sum(r * r, axis=1) for r in residuals)
    products = sum(jnp.sum(r * s, axis=1) for r, s in zip(residuals, scaled))
    stats, work["step"] = together(jnp.stack([squares, products]), work["step"])
    work["two"] = jnp.stack([work["step"], swap_y(work["step"], 2)])
    other_stats = swap(stats, "c")
    other_stats = jnp.concatenate([other_stats[:, share // 2 :], other_stats[:, : share // 2]], axis=1)
    means = (stats + other_stats) / d
    inv_rms = lax.rsqrt(means[0] + norm_eps)[:, None]
    pull = inv_rms**3 * means[1][:, None]
    grads = [(inv_rms * s - r * pull).astype(BF16) for r, s in zip(residuals, scaled)]

    full = [ring_gather(g, *([] if s else [beside_gather])) for s, g in enumerate(grads)]
    outer_step = own_first(work["eight"], bits)
    new_base = (base - outer_step.astype(F32)).reshape(outer_base.shape)

    grad_rows = jnp.concatenate(grads, axis=1)
    d_resid = joined(grad_rows[: share // 2], swap(grad_rows[share // 2 :], "c"), c)

    flat = by_z.reshape(tokens, 2 * width)

    def weight_part(rows, grad):
        return lax.dot_general(rows, grad, (((0,), (0,)), ((), ())), preferred_element_type=F32).astype(BF16)

    def heads_part(grad, span):
        return lax.dot_general(grad, weight[:, span], (((1,), (1,)), ((), ())), preferred_element_type=F32)

    grads_w = [weight_part(flat, g) for g in full]
    others = [swap(g[width:], "c") for g in grads_w]
    weight_grad = joined(
        jnp.concatenate([g[:width] for g in grads_w], axis=1), jnp.concatenate(others, axis=1), c
    )
    head_rows = sum(heads_part(g, s) for g, s in zip(full, cuts))
    head_rows = absolute(head_rows.reshape(NZ, 2, share, 2 * width).transpose(1, 0, 2, 3), 1, z)
    head_rows = absolute(absolute(head_rows.reshape(2, NZ, 2, share // 2, 2 * width), 0, xh), 2, c)
    head_rows = head_rows.reshape(tokens, 2 * width)
    d_heads = (head_rows[:, :width] + swap(head_rows[:, width:].astype(BF16), "c").astype(F32)).astype(BF16)
    return d_resid, d_heads, weight_grad[None], new_base, work["momentum"].reshape(momentum.shape)


def solution(mesh):
    fine = Mesh(mesh.devices.reshape(2, 4, 2, NZ, 2), AXES)
    rep, tp = REP, ("xh", "z", "c")
    return jax.shard_map(
        per_device,
        mesh=fine,
        in_specs=(
            P(AXES, None),
            P(rep, tp),
            P(tp, None),
            P(),
            P(AXES, None),
            P(rep, tp),
            P(tp),
            P(tp, rep, None),
        ),
        out_specs=(P(AXES, None), P(rep, tp), P(rep, tp, None), P(tp), P(tp, rep, None)),
        check_vma=False,
    )
```

```python
import jax
import jax.numpy as jnp
from jax import lax
from jax.sharding import Mesh
from jax.sharding import PartitionSpec as P

norm_eps = 1e-05
outer_rate = 0.7
momentum_coef = 0.9

AXES = ("xl", "y", "xh", "z", "c")
REP = ("xl", "y")
F32 = jnp.float32
BF16 = jnp.bfloat16
NZ = 8
STREAMS = 2


def shift(x, axis, step):
    n = lax.axis_size(axis)
    return lax.ppermute(x, axis, [(i, (i + step) % n) for i in range(n)])


def swap(x, axis):
    return shift(x, axis, 1)


def dot(a, b):
    return jnp.dot(a, b, preferred_element_type=F32)


def together(*xs):
    return lax.optimization_barrier(xs)


def relative(x, axis, at):
    return lax.dynamic_slice_in_dim(jnp.concatenate([x, x], axis=axis), at, x.shape[axis], axis)


def absolute(x, axis, at):
    n = x.shape[axis]
    return lax.dynamic_slice_in_dim(jnp.concatenate([x, x], axis=axis), (n - at) % n, n, axis)


def my_half(x, c):
    n = x.shape[-1] // 2
    return lax.dynamic_slice_in_dim(x, c * n, n, x.ndim - 1)


def joined(mine, other, c):
    first = jnp.where(c == 0, mine, other)
    second = jnp.where(c == 0, other, mine)
    return jnp.concatenate([first, second], axis=1)


def reduce_step(up, down, at_up, at_down, step):
    half = at_up.shape[1] // 2
    if step == 4:
        at_up, at_down = at_up[:, :half], at_down[:, half:]
    elif step == 3:
        at_up = jnp.concatenate([at_up[:, :half] + up.astype(F32), at_up[:, half:]], axis=1)
        at_down = jnp.concatenate([at_down[:, :half], at_down[:, half:] + down.astype(F32)], axis=1)
    else:
        at_up = at_up + up.astype(F32)
        at_down = at_down + down.astype(F32)
    return shift(at_up.astype(BF16), "z", 1), shift(at_down.astype(BF16), "z", -1)


def ring_reduce(rows, weight, beside=lambda j, sent: sent):
    up = down = None
    for j in (4, 3, 2, 1):
        up, down = reduce_step(up, down, dot(rows[j], weight), dot(rows[8 - j], weight), j)
        up = beside(j, up)
    total = dot(rows[0], weight) + up.astype(F32) + down.astype(F32)
    share = total.shape[0] // 2
    return total[:share] + swap(total[share:].astype(BF16), "xh").astype(F32)


def ring_gather(own, beside=lambda j, sent: sent):
    own = jnp.concatenate([own, swap(own, "xh")], axis=0)
    half = own.shape[1] // 2
    got = [own] + [None] * 7
    up = down = own
    for j in (1, 2, 3):
        up = shift(up, "z", 1)
        down = shift(down, "z", -1)
        up = beside(j, up)
        got[8 - j], got[j] = up, down
    left = shift(up[:, :half], "z", 1)
    right = shift(down[:, half:], "z", -1)
    got[4] = jnp.concatenate([left, right], axis=1)
    return jnp.concatenate(got, axis=0)


def own_first(x, bits):
    for axis, bit in enumerate(bits):
        x = jnp.where(bit == 0, x, jnp.flip(x, axis))
    return x


def swap_y(x, bit):
    return lax.ppermute(x, "y", [(i, i ^ bit) for i in range(4)])


def per_device(inputs, heads_out, out_weight, norm_gain, cotangent, inner_params, outer_base, momentum):
    c, z, xh = lax.axis_index("c"), lax.axis_index("z"), lax.axis_index("xh")
    tokens, width = heads_out.shape
    d = out_weight.shape[1]
    share = tokens // (2 * NZ)
    p = d // 2 // STREAMS
    cuts = [slice(s * p, (s + 1) * p) for s in range(STREAMS)]

    replicas = lax.axis_size("xl") * lax.axis_size("y")
    block = (2, 2, 2, outer_base.shape[0] // (replicas * 128), 128)
    xl, y = lax.axis_index("xl"), lax.axis_index("y")
    bits = (xl, y // 2, y % 2)
    base = outer_base.reshape(block)
    momentum_rows = momentum.reshape(block[3:])
    difference = own_first((base - inner_params.reshape(block)).astype(BF16), bits)
    work = {"x": swap(difference[1], "xl")}

    def beside_reduce(j, up):
        if j == 4:
            up, work["x"] = together(up, work["x"])
            work["pair"] = difference[0].astype(F32) + work["x"].astype(F32)
            work["y"] = swap_y(work["pair"][:, 1].astype(BF16), 1)
        elif j == 2:
            up, work["y"] = together(up, work["y"])
            quad = work["pair"][:, 0] + work["y"].astype(F32)
            work["total"] = quad[0], swap_y(quad[1].astype(BF16), 2)
        elif j == 1:
            own_total, other_total = work["total"]
            up, other_total = together(up, other_total)
            mean_delta = (own_total + other_total.astype(F32)) / replicas
            new_momentum = momentum_coef * momentum_rows + mean_delta
            work["momentum"] = new_momentum
            work["step"] = (outer_rate * (mean_delta + momentum_coef * new_momentum)).astype(BF16)
        return up

    def beside_gather(j, up):
        if j == 1:
            up, work["two"] = together(up, work["two"])
            work["four"] = jnp.stack([work["two"], swap_y(work["two"], 1)], axis=1)
        elif j == 3:
            up, work["four"] = together(up, work["four"])
            work["eight"] = jnp.stack([work["four"], swap(work["four"], "xl")])
        return up

    def both_rows(mine, other):
        return jnp.concatenate([my_half(mine, c), my_half(other, c)], axis=0)

    weight = both_rows(out_weight, swap(out_weight, "c"))
    heads = jnp.concatenate([heads_out, swap(heads_out, "c")], axis=1)
    by_x = heads.reshape(2, NZ, 2, share // 2, 2 * width)
    by_x = relative(relative(by_x, 0, xh), 2, c).reshape(2, NZ, share, 2 * width)
    by_z = relative(by_x, 1, z).transpose(1, 0, 2, 3).reshape(NZ, 2 * share, 2 * width)
    other_inputs, other_cotangent = swap(inputs, "c"), swap(cotangent, "c")
    gain = my_half(norm_gain, c)

    rows = [by_z[j] for j in range(NZ)]
    rows[3], other_inputs, other_cotangent = together(rows[3], other_inputs, other_cotangent)
    pieces = [ring_reduce(rows, weight[:, cut], *([] if s else [beside_reduce])) for s, cut in enumerate(cuts)]

    inputs, cotangent = both_rows(inputs, other_inputs), both_rows(cotangent, other_cotangent)
    residuals = [inputs[:, s].astype(F32) + piece for s, piece in zip(cuts, pieces)]
    scaled = [gain[None, s] * cotangent[:, s].astype(F32) for s in cuts]
    squares = sum(jnp.sum(r * r, axis=1) for r in residuals)
    products = sum(jnp.sum(r * s, axis=1) for r, s in zip(residuals, scaled))
    stats, work["step"] = together(jnp.stack([squares, products]), work["step"])
    work["two"] = jnp.stack([work["step"], swap_y(work["step"], 2)])
    other_stats = swap(stats, "c")
    other_stats = jnp.concatenate([other_stats[:, share // 2 :], other_stats[:, : share // 2]], axis=1)
    means = (stats + other_stats) / d
    inv_rms = lax.rsqrt(means[0] + norm_eps)[:, None]
    pull = inv_rms**3 * means[1][:, None]
    grads = [(inv_rms * s - r * pull).astype(BF16) for r, s in zip(residuals, scaled)]

    full = [ring_gather(g, *([beside_gather] if s else [])) for s, g in enumerate(grads)]
    outer_step = own_first(work["eight"], bits)
    new_base = (base - outer_step.astype(F32)).reshape(outer_base.shape)

    grad_rows = jnp.concatenate(grads, axis=1)
    d_resid = joined(grad_rows[: share // 2], swap(grad_rows[share // 2 :], "c"), c)

    flat = by_z.reshape(tokens, 2 * width)

    def weight_part(rows, grad):
        return lax.dot_general(rows, grad, (((0,), (0,)), ((), ())), preferred_element_type=F32).astype(BF16)

    def heads_part(grad, span):
        return lax.dot_general(grad, weight[:, span], (((1,), (1,)), ((), ())), preferred_element_type=F32)

    grads_w = [weight_part(flat, g) for g in full]
    others = [swap(g[width:], "c") for g in grads_w]
    weight_grad = joined(
        jnp.concatenate([g[:width] for g in grads_w], axis=1), jnp.concatenate(others, axis=1), c
    )
    head_rows = sum(heads_part(g, s) for g, s in zip(full, cuts))
    head_rows = absolute(head_rows.reshape(NZ, 2, share, 2 * width).transpose(1, 0, 2, 3), 1, z)
    head_rows = absolute(absolute(head_rows.reshape(2, NZ, 2, share // 2, 2 * width), 0, xh), 2, c)
    head_rows = head_rows.reshape(tokens, 2 * width)
    d_heads = (head_rows[:, :width] + swap(head_rows[:, width:].astype(BF16), "c").astype(F32)).astype(BF16)
    return d_resid, d_heads, weight_grad[None], new_base, work["momentum"].reshape(momentum.shape)


def solution(mesh):
    fine = Mesh(mesh.devices.reshape(2, 4, 2, NZ, 2), AXES)
    rep, tp = REP, ("xh", "z", "c")
    return jax.shard_map(
        per_device,
        mesh=fine,
        in_specs=(
            P(AXES, None),
            P(rep, tp),
            P(tp, None),
            P(),
            P(AXES, None),
            P(rep, tp),
            P(tp),
            P(tp, rep, None),
        ),
        out_specs=(P(AXES, None), P(rep, tp), P(rep, tp, None), P(tp), P(tp, rep, None)),
        check_vma=False,
    )
```

```python
import jax
import jax.numpy as jnp
from jax import lax
from jax.sharding import Mesh
from jax.sharding import PartitionSpec as P

norm_eps = 1e-05
outer_rate = 0.7
momentum_coef = 0.9

AXES = ("xl", "y", "xh", "z", "c")
REP = ("xl", "y")
F32 = jnp.float32
BF16 = jnp.bfloat16
NZ = 8
STREAMS = 2


def shift(x, axis, step):
    n = lax.axis_size(axis)
    return lax.ppermute(x, axis, [(i, (i + step) % n) for i in range(n)])


def swap(x, axis):
    return shift(x, axis, 1)


def dot(a, b):
    return jnp.dot(a, b, preferred_element_type=F32)


def together(*xs):
    return lax.optimization_barrier(xs)


def relative(x, axis, at):
    return lax.dynamic_slice_in_dim(jnp.concatenate([x, x], axis=axis), at, x.shape[axis], axis)


def absolute(x, axis, at):
    n = x.shape[axis]
    return lax.dynamic_slice_in_dim(jnp.concatenate([x, x], axis=axis), (n - at) % n, n, axis)


def my_half(x, c):
    n = x.shape[-1] // 2
    return lax.dynamic_slice_in_dim(x, c * n, n, x.ndim - 1)


def joined(mine, other, c):
    first = jnp.where(c == 0, mine, other)
    second = jnp.where(c == 0, other, mine)
    return jnp.concatenate([first, second], axis=1)


def reduce_step(up, down, at_up, at_down, step):
    half = at_up.shape[1] // 2
    if step == 4:
        at_up, at_down = at_up[:, :half], at_down[:, half:]
    elif step == 3:
        at_up = jnp.concatenate([at_up[:, :half] + up.astype(F32), at_up[:, half:]], axis=1)
        at_down = jnp.concatenate([at_down[:, :half], at_down[:, half:] + down.astype(F32)], axis=1)
    else:
        at_up = at_up + up.astype(F32)
        at_down = at_down + down.astype(F32)
    return shift(at_up.astype(BF16), "z", 1), shift(at_down.astype(BF16), "z", -1)


def ring_reduce(rows, weight, beside=lambda j, sent: sent):
    up = down = None
    for j in (4, 3, 2, 1):
        up, down = reduce_step(up, down, dot(rows[j], weight), dot(rows[8 - j], weight), j)
        up = beside(j, up)
        if j == 4:
            rows = list(rows)
            up, rows[3], rows[5] = together(up, rows[3], rows[5])
    total = dot(rows[0], weight) + up.astype(F32) + down.astype(F32)
    share = total.shape[0] // 2
    return total[:share] + swap(total[share:].astype(BF16), "xh").astype(F32)


def ring_gather(own, beside=lambda j, sent: sent):
    own = jnp.concatenate([own, swap(own, "xh")], axis=0)
    half = own.shape[1] // 2
    got = [own] + [None] * 7
    up = down = own
    for j in (1, 2, 3):
        up = shift(up, "z", 1)
        down = shift(down, "z", -1)
        up = beside(j, up)
        got[8 - j], got[j] = up, down
    left = shift(up[:, :half], "z", 1)
    right = shift(down[:, half:], "z", -1)
    got[4] = jnp.concatenate([left, right], axis=1)
    return jnp.concatenate(got, axis=0)


def own_first(x, bits):
    for axis, bit in enumerate(bits):
        x = jnp.where(bit == 0, x, jnp.flip(x, axis))
    return x


def swap_y(x, bit):
    return lax.ppermute(x, "y", [(i, i ^ bit) for i in range(4)])


def per_device(inputs, heads_out, out_weight, norm_gain, cotangent, inner_params, outer_base, momentum):
    c, z, xh = lax.axis_index("c"), lax.axis_index("z"), lax.axis_index("xh")
    tokens, width = heads_out.shape
    d = out_weight.shape[1]
    share = tokens // (2 * NZ)
    p = d // 2 // STREAMS
    cuts = [slice(s * p, (s + 1) * p) for s in range(STREAMS)]

    replicas = lax.axis_size("xl") * lax.axis_size("y")
    block = (2, 2, 2, outer_base.shape[0] // (replicas * 128), 128)
    xl, y = lax.axis_index("xl"), lax.axis_index("y")
    bits = (xl, y // 2, y % 2)
    base = outer_base.reshape(block)
    momentum_rows = momentum.reshape(block[3:])
    difference = own_first((base - inner_params.reshape(block)).astype(BF16), bits)
    work = {"x": swap(difference[1], "xl")}

    def beside_reduce(j, up):
        if j == 4:
            up, work["x"], *work["rows"] = together(up, work["x"], *work["rows"])
            work["pair"] = difference[0].astype(F32) + work["x"].astype(F32)
            work["y"] = swap_y(work["pair"][:, 1].astype(BF16), 1)
        elif j == 2:
            up, work["y"], *work["late"] = together(up, work["y"], inputs, cotangent, norm_gain)
            quad = work["pair"][:, 0] + work["y"].astype(F32)
            work["total"] = quad[0], swap_y(quad[1].astype(BF16), 2)
        elif j == 1:
            own_total, other_total = work["total"]
            up, other_total = together(up, other_total)
            mean_delta = (own_total + other_total.astype(F32)) / replicas
            new_momentum = momentum_coef * momentum_rows + mean_delta
            work["momentum"] = new_momentum
            work["step"] = (outer_rate * (mean_delta + momentum_coef * new_momentum)).astype(BF16)
        return up

    def beside_gather(j, up):
        if j == 1:
            up, work["step"] = together(up, work["step"])
            work["other"] = swap_y(work["step"], 2)
        elif j == 2:
            up, other = together(up, work["other"])
            work["two"] = jnp.stack([work["step"], other])
            work["other"] = swap_y(work["two"], 1)
        elif j == 3:
            up, other = together(up, work["other"])
            work["four"] = jnp.stack([work["two"], other], axis=1)
            work["eight"] = jnp.stack([work["four"], swap(work["four"], "xl")])
        return up

    def both_rows(mine, other):
        return jnp.concatenate([my_half(mine, c), my_half(other, c)], axis=0)

    other_weight, other_heads = swap(out_weight, "c"), swap(heads_out, "c")
    work["rows"] = swap(inputs, "c"), swap(cotangent, "c")

    def weight_columns(cut):
        return jnp.concatenate(
            [lax.dynamic_slice_in_dim(w, c * (d // 2) + cut.start, p, 1) for w in (out_weight, other_weight)], axis=0
        )

    weights = [weight_columns(cut) for cut in cuts]
    heads = jnp.concatenate([heads_out, other_heads], axis=1)
    by_x = heads.reshape(2, NZ, 2, share // 2, 2 * width)
    by_x = relative(relative(by_x, 0, xh), 2, c).reshape(2, NZ, share, 2 * width)
    by_z = relative(by_x, 1, z).transpose(1, 0, 2, 3).reshape(NZ, 2 * share, 2 * width)

    rows = [by_z[j] for j in range(NZ)]
    pieces = [ring_reduce(rows, w, *([] if s else [beside_reduce])) for s, w in enumerate(weights)]

    *own_rows, gain = work["late"]
    inputs, cotangent = [both_rows(*pair) for pair in zip(own_rows, work["rows"])]
    gain = my_half(gain, c)
    residuals = [inputs[:, s].astype(F32) + piece for s, piece in zip(cuts, pieces)]
    scaled = [gain[None, s] * cotangent[:, s].astype(F32) for s in cuts]
    squares = sum(jnp.sum(r * r, axis=1) for r in residuals)
    products = sum(jnp.sum(r * s, axis=1) for r, s in zip(residuals, scaled))
    stats = jnp.stack([squares, products])
    other_stats = swap(stats, "c")
    other_stats = jnp.concatenate([other_stats[:, share // 2 :], other_stats[:, : share // 2]], axis=1)
    means = (stats + other_stats) / d
    inv_rms = lax.rsqrt(means[0] + norm_eps)[:, None]
    pull = inv_rms**3 * means[1][:, None]
    grads = [(inv_rms * s - r * pull).astype(BF16) for r, s in zip(residuals, scaled)]

    full = [ring_gather(g, *([beside_gather] if s else [])) for s, g in enumerate(grads)]
    outer_step = own_first(work["eight"], bits)
    new_base = (base - outer_step.astype(F32)).reshape(outer_base.shape)

    grad_rows = jnp.concatenate(grads, axis=1)
    d_resid = joined(grad_rows[: share // 2], swap(grad_rows[share // 2 :], "c"), c)

    flat = by_z.reshape(tokens, 2 * width)

    def weight_part(rows, grad):
        return lax.dot_general(rows, grad, (((0,), (0,)), ((), ())), preferred_element_type=F32).astype(BF16)

    def heads_part(grad, weight):
        return lax.dot_general(grad, weight, (((1,), (1,)), ((), ())), preferred_element_type=F32)

    grads_w = [weight_part(flat, g) for g in full]
    others = [swap(g[width:], "c") for g in grads_w]
    weight_grad = joined(
        jnp.concatenate([g[:width] for g in grads_w], axis=1), jnp.concatenate(others, axis=1), c
    )
    head_rows = sum(heads_part(g, w) for g, w in zip(full, weights))
    head_rows = absolute(head_rows.reshape(NZ, 2, share, 2 * width).transpose(1, 0, 2, 3), 1, z)
    head_rows = absolute(absolute(head_rows.reshape(2, NZ, 2, share // 2, 2 * width), 0, xh), 2, c)
    head_rows = head_rows.reshape(tokens, 2 * width)
    d_heads = (head_rows[:, :width] + swap(head_rows[:, width:].astype(BF16), "c").astype(F32)).astype(BF16)
    return d_resid, d_heads, weight_grad[None], new_base, work["momentum"].reshape(momentum.shape)


def solution(mesh):
    fine = Mesh(mesh.devices.reshape(2, 4, 2, NZ, 2), AXES)
    rep, tp = REP, ("xh", "z", "c")
    return jax.shard_map(
        per_device,
        mesh=fine,
        in_specs=(
            P(AXES, None),
            P(rep, tp),
            P(tp, None),
            P(),
            P(AXES, None),
            P(rep, tp),
            P(tp),
            P(tp, rep, None),
        ),
        out_specs=(P(AXES, None), P(rep, tp), P(rep, tp, None), P(tp), P(tp, rep, None)),
        check_vma=False,
    )
```

```python
import jax
import jax.numpy as jnp
from jax import lax
from jax.sharding import Mesh
from jax.sharding import PartitionSpec as P

norm_eps = 1e-05
outer_rate = 0.7
momentum_coef = 0.9

AXES = ("xl", "y", "xh", "z", "c")
REP = ("xl", "y")
F32 = jnp.float32
BF16 = jnp.bfloat16
NZ = 8
STREAMS = 2


def shift(x, axis, step):
    n = lax.axis_size(axis)
    return lax.ppermute(x, axis, [(i, (i + step) % n) for i in range(n)])


def swap(x, axis):
    return shift(x, axis, 1)


def dot(a, b):
    return jnp.dot(a, b, preferred_element_type=F32)


def together(*xs):
    return lax.optimization_barrier(xs)


def relative(x, axis, at):
    return lax.dynamic_slice_in_dim(jnp.concatenate([x, x], axis=axis), at, x.shape[axis], axis)


def absolute(x, axis, at):
    n = x.shape[axis]
    return lax.dynamic_slice_in_dim(jnp.concatenate([x, x], axis=axis), (n - at) % n, n, axis)


def my_half(x, c):
    n = x.shape[-1] // 2
    return lax.dynamic_slice_in_dim(x, c * n, n, x.ndim - 1)


def joined(mine, other, c):
    first = jnp.where(c == 0, mine, other)
    second = jnp.where(c == 0, other, mine)
    return jnp.concatenate([first, second], axis=1)


def ring_reduce(rows, weight, lead, beside=lambda j, sent: sent):
    way = {1: 0, -1: 0}
    for j in (4, 3, 2, 1):
        for step in (1, -1):
            if j < 4 or step == lead:
                part = dot(rows[j if step == 1 else (8 - j)], weight) + way[step]
                way[step] = shift(part.astype(BF16), "z", step)
        way[lead] = beside(j, way[lead])
        way = {step: sent.astype(F32) if j < 4 or step == lead else 0 for step, sent in way.items()}
    total = dot(rows[0], weight) + way[1] + way[-1]
    share = total.shape[0] // 2
    return total[:share] + swap(total[share:].astype(BF16), "xh").astype(F32)


def ring_gather(own, lead, beside=lambda j, sent: sent):
    own = jnp.concatenate([own, swap(own, "xh")], axis=0)
    got = [own] + [None] * 7
    up = down = own
    for j in (1, 2, 3):
        up = shift(up, "z", 1)
        down = shift(down, "z", -1)
        up = beside(j, up)
        got[8 - j], got[j] = up, down
    got[4] = shift(up, "z", 1) if lead == 1 else shift(down, "z", -1)
    return jnp.concatenate(got, axis=0)


def own_first(x, bits):
    for axis, bit in enumerate(bits):
        x = jnp.where(bit == 0, x, jnp.flip(x, axis))
    return x


def swap_y(x, bit):
    return lax.ppermute(x, "y", [(i, i ^ bit) for i in range(4)])


def per_device(inputs, heads_out, out_weight, norm_gain, cotangent, inner_params, outer_base, momentum):
    c, z, xh = lax.axis_index("c"), lax.axis_index("z"), lax.axis_index("xh")
    tokens, width = heads_out.shape
    d = out_weight.shape[1]
    share = tokens // (2 * NZ)
    p = d // 2 // STREAMS
    cuts = [slice(s * p, (s + 1) * p) for s in range(STREAMS)]

    replicas = lax.axis_size("xl") * lax.axis_size("y")
    block = (2, 2, 2, outer_base.shape[0] // (replicas * 128), 128)
    xl, y = lax.axis_index("xl"), lax.axis_index("y")
    bits = (xl, y // 2, y % 2)
    base = outer_base.reshape(block)
    momentum_rows = momentum.reshape(block[3:])
    difference = own_first((base - inner_params.reshape(block)).astype(BF16), bits)
    work = {"x": swap(difference[1], "xl")}

    def beside_reduce(j, up):
        if j == 4:
            up, work["x"], *work["rows"] = together(up, work["x"], *work["rows"])
            work["pair"] = difference[0].astype(F32) + work["x"].astype(F32)
            work["y"] = swap_y(work["pair"][:, 1].astype(BF16), 1)
        elif j == 2:
            up, work["y"], *work["late"] = together(up, work["y"], inputs, cotangent, norm_gain)
            quad = work["pair"][:, 0] + work["y"].astype(F32)
            work["total"] = quad[0], swap_y(quad[1].astype(BF16), 2)
        elif j == 1:
            own_total, other_total = work["total"]
            up, other_total = together(up, other_total)
            mean_delta = (own_total + other_total.astype(F32)) / replicas
            new_momentum = momentum_coef * momentum_rows + mean_delta
            work["momentum"] = new_momentum
            work["step"] = (outer_rate * (mean_delta + momentum_coef * new_momentum)).astype(BF16)
        return up

    def beside_gather(j, up):
        if j == 1:
            up, work["step"] = together(up, work["step"])
            work["other"] = swap_y(work["step"], 2)
        elif j == 2:
            up, other = together(up, work["other"])
            work["two"] = jnp.stack([work["step"], other])
            work["other"] = swap_y(work["two"], 1)
        elif j == 3:
            up, other = together(up, work["other"])
            work["four"] = jnp.stack([work["two"], other], axis=1)
            work["eight"] = jnp.stack([work["four"], swap(work["four"], "xl")])
        return up

    def both_rows(mine, other):
        return jnp.concatenate([my_half(mine, c), my_half(other, c)], axis=0)

    other_weight, other_heads = swap(out_weight, "c"), swap(heads_out, "c")
    work["rows"] = swap(inputs, "c"), swap(cotangent, "c")

    def weight_columns(cut):
        return jnp.concatenate(
            [lax.dynamic_slice_in_dim(w, c * (d // 2) + cut.start, p, 1) for w in (out_weight, other_weight)], axis=0
        )

    weights = [weight_columns(cut) for cut in cuts]
    heads = jnp.concatenate([heads_out, other_heads], axis=1)
    by_x = heads.reshape(2, NZ, 2, share // 2, 2 * width)
    by_x = relative(relative(by_x, 0, xh), 2, c).reshape(2, NZ, share, 2 * width)
    by_z = relative(by_x, 1, z).transpose(1, 0, 2, 3).reshape(NZ, 2 * share, 2 * width)

    rows = [by_z[j] for j in range(NZ)]
    pieces = [ring_reduce(rows, w, *([-1] if s else [1, beside_reduce])) for s, w in enumerate(weights)]

    *own_rows, gain = work["late"]
    inputs, cotangent = [both_rows(*pair) for pair in zip(own_rows, work["rows"])]
    gain = my_half(gain, c)
    residuals = [inputs[:, s].astype(F32) + piece for s, piece in zip(cuts, pieces)]
    scaled = [gain[None, s] * cotangent[:, s].astype(F32) for s in cuts]
    squares = sum(jnp.sum(r * r, axis=1) for r in residuals)
    products = sum(jnp.sum(r * s, axis=1) for r, s in zip(residuals, scaled))
    stats = jnp.stack([squares, products])
    other_stats = swap(stats, "c")
    other_stats = jnp.concatenate([other_stats[:, share // 2 :], other_stats[:, : share // 2]], axis=1)
    means = (stats + other_stats) / d
    inv_rms = lax.rsqrt(means[0] + norm_eps)[:, None]
    pull = inv_rms**3 * means[1][:, None]
    grads = [(inv_rms * s - r * pull).astype(BF16) for r, s in zip(residuals, scaled)]

    full = [ring_gather(g, *([1, beside_gather] if s else [-1])) for s, g in enumerate(grads)]
    outer_step = own_first(work["eight"], bits)
    new_base = (base - outer_step.astype(F32)).reshape(outer_base.shape)

    grad_rows = jnp.concatenate(grads, axis=1)
    d_resid = joined(grad_rows[: share // 2], swap(grad_rows[share // 2 :], "c"), c)

    flat = by_z.reshape(tokens, 2 * width)

    def weight_part(rows, grad):
        return lax.dot_general(rows, grad, (((0,), (0,)), ((), ())), preferred_element_type=F32).astype(BF16)

    def heads_part(grad, weight):
        return lax.dot_general(grad, weight, (((1,), (1,)), ((), ())), preferred_element_type=F32)

    grads_w = [weight_part(flat, g) for g in full]
    others = [swap(g[width:], "c") for g in grads_w]
    weight_grad = joined(
        jnp.concatenate([g[:width] for g in grads_w], axis=1), jnp.concatenate(others, axis=1), c
    )
    head_rows = sum(heads_part(g, w) for g, w in zip(full, weights))
    head_rows = absolute(head_rows.reshape(NZ, 2, share, 2 * width).transpose(1, 0, 2, 3), 1, z)
    head_rows = absolute(absolute(head_rows.reshape(2, NZ, 2, share // 2, 2 * width), 0, xh), 2, c)
    head_rows = head_rows.reshape(tokens, 2 * width)
    d_heads = (head_rows[:, :width] + swap(head_rows[:, width:].astype(BF16), "c").astype(F32)).astype(BF16)
    return d_resid, d_heads, weight_grad[None], new_base, work["momentum"].reshape(momentum.shape)


def solution(mesh):
    fine = Mesh(mesh.devices.reshape(2, 4, 2, NZ, 2), AXES)
    rep, tp = REP, ("xh", "z", "c")
    return jax.shard_map(
        per_device,
        mesh=fine,
        in_specs=(
            P(AXES, None),
            P(rep, tp),
            P(tp, None),
            P(),
            P(AXES, None),
            P(rep, tp),
            P(tp),
            P(tp, rep, None),
        ),
        out_specs=(P(AXES, None), P(rep, tp), P(rep, tp, None), P(tp), P(tp, rep, None)),
        check_vma=False,
    )
```

```python
import jax
import jax.numpy as jnp
from jax import lax
from jax.sharding import Mesh
from jax.sharding import PartitionSpec as P

norm_eps = 1e-05
outer_rate = 0.7
momentum_coef = 0.9

AXES = ("xl", "y", "xh", "z", "c")
REP = ("xl", "y")
F32 = jnp.float32
BF16 = jnp.bfloat16
NZ = 8
STREAMS = 2


def shift(x, axis, step):
    n = lax.axis_size(axis)
    return lax.ppermute(x, axis, [(i, (i + step) % n) for i in range(n)])


def swap(x, axis):
    return shift(x, axis, 1)


def dot(a, b):
    return jnp.dot(a, b, preferred_element_type=F32)


def together(*xs):
    return lax.optimization_barrier(xs)


def relative(x, axis, at):
    return lax.dynamic_slice_in_dim(jnp.concatenate([x, x], axis=axis), at, x.shape[axis], axis)


def absolute(x, axis, at):
    n = x.shape[axis]
    return lax.dynamic_slice_in_dim(jnp.concatenate([x, x], axis=axis), (n - at) % n, n, axis)


def my_half(x, c):
    n = x.shape[-1] // 2
    return lax.dynamic_slice_in_dim(x, c * n, n, x.ndim - 1)


def joined(mine, other, c):
    first = jnp.where(c == 0, mine, other)
    second = jnp.where(c == 0, other, mine)
    return jnp.concatenate([first, second], axis=1)


def ring_reduce(rows, weight, lead, beside=lambda j, sent: sent):
    way = {1: 0, -1: 0}
    for j in (4, 3, 2, 1):
        for step in (1, -1):
            if j < 4 or step == lead:
                part = dot(rows[j if step == 1 else (8 - j)], weight) + way[step]
                way[step] = shift(part.astype(BF16), "z", step)
        way[lead] = beside(j, way[lead])
        way = {step: sent.astype(F32) if j < 4 or step == lead else 0 for step, sent in way.items()}
    total = dot(rows[0], weight) + way[1] + way[-1]
    share = total.shape[0] // 2
    return total[:share] + swap(total[share:].astype(BF16), "xh").astype(F32)


def ring_gather(own, lead, beside=lambda j, sent: sent):
    own = jnp.concatenate([own, swap(own, "xh")], axis=0)
    got = [own] + [None] * 7
    up = down = own
    for j in (1, 2, 3):
        up = shift(up, "z", 1)
        down = shift(down, "z", -1)
        up = beside(j, up)
        got[8 - j], got[j] = up, down
    got[4] = shift(up, "z", 1) if lead == 1 else shift(down, "z", -1)
    return jnp.concatenate(got, axis=0)


def own_first(x, bits):
    for axis, bit in enumerate(bits):
        x = jnp.where(bit == 0, x, jnp.flip(x, axis))
    return x


def swap_y(x, bit):
    return lax.ppermute(x, "y", [(i, i ^ bit) for i in range(4)])


def per_device(inputs, heads_out, out_weight, norm_gain, cotangent, inner_params, outer_base, momentum):
    c, z, xh = lax.axis_index("c"), lax.axis_index("z"), lax.axis_index("xh")
    tokens, width = heads_out.shape
    d = out_weight.shape[1]
    share = tokens // (2 * NZ)
    p = d // 2 // STREAMS
    cuts = [slice(s * p, (s + 1) * p) for s in range(STREAMS)]

    replicas = lax.axis_size("xl") * lax.axis_size("y")
    block = (2, 2, 2, outer_base.shape[0] // (replicas * 128), 128)
    xl, y = lax.axis_index("xl"), lax.axis_index("y")
    bits = (xl, y // 2, y % 2)
    base = outer_base.reshape(block)
    momentum_rows = momentum.reshape(block[3:])
    difference = own_first((base - inner_params.reshape(block)).astype(BF16), bits)
    work = {"x": swap(difference[1], "xl")}

    def beside_reduce(j, up):
        if j == 4:
            up, work["x"], *work["rows"] = together(up, work["x"], *work["rows"])
            work["pair"] = difference[0].astype(F32) + work["x"].astype(F32)
            work["y"] = swap_y(work["pair"][:, 1].astype(BF16), 1)
        elif j == 2:
            up, work["y"], *work["late"] = together(up, work["y"], inputs, cotangent, norm_gain)
            quad = work["pair"][:, 0] + work["y"].astype(F32)
            work["quad"] = quad[0], quad[1].astype(BF16)
        return up

    def beside_second(j, sent):
        if j == 2:
            own_total, other_total = work["quad"]
            sent, other_total = together(sent, other_total)
            work["total"] = own_total, swap_y(other_total, 2)
        elif j == 1:
            own_total, other_total = work["total"]
            sent, other_total = together(sent, other_total)
            mean_delta = (own_total + other_total.astype(F32)) / replicas
            new_momentum = momentum_coef * momentum_rows + mean_delta
            work["momentum"] = new_momentum
            work["step"] = (outer_rate * (mean_delta + momentum_coef * new_momentum)).astype(BF16)
        return sent

    def beside_gather(j, up):
        if j == 1:
            up, work["step"] = together(up, work["step"])
            work["other"] = swap_y(work["step"], 2)
        elif j == 2:
            up, other = together(up, work["other"])
            work["two"] = jnp.stack([work["step"], other])
            work["other"] = swap_y(work["two"], 1)
        elif j == 3:
            up, other = together(up, work["other"])
            work["four"] = jnp.stack([work["two"], other], axis=1)
            work["eight"] = jnp.stack([work["four"], swap(work["four"], "xl")])
        return up

    def both_rows(mine, other):
        return jnp.concatenate([my_half(mine, c), my_half(other, c)], axis=0)

    other_weight, other_heads = swap(out_weight, "c"), swap(heads_out, "c")
    work["rows"] = swap(inputs, "c"), swap(cotangent, "c")

    def weight_columns(cut):
        return jnp.concatenate(
            [lax.dynamic_slice_in_dim(w, c * (d // 2) + cut.start, p, 1) for w in (out_weight, other_weight)], axis=0
        )

    weights = [weight_columns(cut) for cut in cuts]
    heads = jnp.concatenate([heads_out, other_heads], axis=1)
    by_x = heads.reshape(2, NZ, 2, share // 2, 2 * width)
    by_x = relative(relative(by_x, 0, xh), 2, c).reshape(2, NZ, share, 2 * width)
    by_z = relative(by_x, 1, z).transpose(1, 0, 2, 3).reshape(NZ, 2 * share, 2 * width)

    rows = [by_z[j] for j in range(NZ)]
    pieces = [ring_reduce(rows, w, *([-1, beside_second] if s else [1, beside_reduce])) for s, w in enumerate(weights)]

    *own_rows, gain = work["late"]
    inputs, cotangent = [both_rows(*pair) for pair in zip(own_rows, work["rows"])]
    gain = my_half(gain, c)
    residuals = [inputs[:, s].astype(F32) + piece for s, piece in zip(cuts, pieces)]
    scaled = [gain[None, s] * cotangent[:, s].astype(F32) for s in cuts]
    squares = sum(jnp.sum(r * r, axis=1) for r in residuals)
    products = sum(jnp.sum(r * s, axis=1) for r, s in zip(residuals, scaled))
    stats = jnp.stack([squares, products])
    other_stats = swap(stats, "c")
    other_stats = jnp.concatenate([other_stats[:, share // 2 :], other_stats[:, : share // 2]], axis=1)
    means = (stats + other_stats) / d
    inv_rms = lax.rsqrt(means[0] + norm_eps)[:, None]
    pull = inv_rms**3 * means[1][:, None]
    grads = [(inv_rms * s - r * pull).astype(BF16) for r, s in zip(residuals, scaled)]

    full = [ring_gather(g, *([1, beside_gather] if s else [-1])) for s, g in enumerate(grads)]
    outer_step = own_first(work["eight"], bits)
    new_base = (base - outer_step.astype(F32)).reshape(outer_base.shape)

    grad_rows = jnp.concatenate(grads, axis=1)
    d_resid = joined(grad_rows[: share // 2], swap(grad_rows[share // 2 :], "c"), c)

    flat = by_z.reshape(tokens, 2 * width)

    def weight_part(rows, grad):
        return lax.dot_general(rows, grad, (((0,), (0,)), ((), ())), preferred_element_type=F32).astype(BF16)

    def heads_part(grad, weight):
        return lax.dot_general(grad, weight, (((1,), (1,)), ((), ())), preferred_element_type=F32)

    grads_w = [weight_part(flat, g) for g in full]
    others = [swap(g[width:], "c") for g in grads_w]
    weight_grad = joined(
        jnp.concatenate([g[:width] for g in grads_w], axis=1), jnp.concatenate(others, axis=1), c
    )
    head_rows = sum(heads_part(g, w) for g, w in zip(full, weights))
    head_rows = absolute(head_rows.reshape(NZ, 2, share, 2 * width).transpose(1, 0, 2, 3), 1, z)
    head_rows = absolute(absolute(head_rows.reshape(2, NZ, 2, share // 2, 2 * width), 0, xh), 2, c)
    head_rows = head_rows.reshape(tokens, 2 * width)
    d_heads = (head_rows[:, :width] + swap(head_rows[:, width:].astype(BF16), "c").astype(F32)).astype(BF16)
    return d_resid, d_heads, weight_grad[None], new_base, work["momentum"].reshape(momentum.shape)


def solution(mesh):
    fine = Mesh(mesh.devices.reshape(2, 4, 2, NZ, 2), AXES)
    rep, tp = REP, ("xh", "z", "c")
    return jax.shard_map(
        per_device,
        mesh=fine,
        in_specs=(
            P(AXES, None),
            P(rep, tp),
            P(tp, None),
            P(),
            P(AXES, None),
            P(rep, tp),
            P(tp),
            P(tp, rep, None),
        ),
        out_specs=(P(AXES, None), P(rep, tp), P(rep, tp, None), P(tp), P(tp, rep, None)),
        check_vma=False,
    )
```
